256 devices in a mesh: dp: 32 (over y, z_hi, core), tensor: 8 (over x, z_lo).
Axes of the slice: x: 4, y: 4, z: 8 (z_hi: 4, z_lo: 2; z = z_hi * 2 + z_lo), core: 2. Of those that a mesh axis runs over, the one named last changes fastest.
Arguments:
- prefix_kv: bfloat16 [65536, 2048], P('dp', 'tensor'), may hold values from -24 to 24
- page_key_values: bfloat16 [1024, 256, 2048], P('dp', None, 'tensor'), may hold values from -6 to 6
- context_len: int32 [1024], P('dp'), may hold values from 1 to 256
- prefill_owner: int32 [1], replicated, may hold values from 0 to 31
- assign: int32 [1024, 1], P('dp'), may hold values from 0 to 31, as said below
- x_new: bfloat16 [1024, 4, 8192], P('dp', None, 'tensor'), may hold values from -6 to 6
- norm_gain: float32 [8192], replicated, may hold values from 0.1 to 1.9
- key_weight: bfloat16 [8192, 1024], P(None, 'tensor'), may hold values from -0.25 to 0.25
- value_weight: bfloat16 [8192, 1024], P(None, 'tensor'), may hold values from -0.0625 to 0.0625
- decoded_queries: bfloat16 [1024, 4, 8192], P('dp', None, 'tensor'), may hold values from -30 to 30
Outputs:
- decoded: bfloat16 [2048, 4, 8192], P('dp', None, 'tensor')
The draws below stay inside these ranges and needn't reach their ends.
Inputs may be any that keep to these rules, and one draw needn't show every extreme that they name: `assign`: within the 32 requests of one device no group is named more than 2 times; one group, the same for every device, is named exactly 2 times by the requests of every device.
All inputs are finite; a program needn't handle non-finite values.
Results may differ from the reference program's by a relative error of at most 0.0088.
Values may be sent and summed in bfloat16 or wider, within the bound.
No kernel may reach another device: no remote copies, remote signals or barrier semaphores. Data moves between devices by JAX's collectives and lax.ppermute only.
A program may use at most 128 MiB of HBM per device.

```python
import math
import jax
import jax.numpy as jnp
from jax import lax

MODEL_WIDTH = 8192
QUERY_HEADS = 64
KV_HEAD_COUNT = 8
HEAD_SIZE = 128
PAGE_POSITIONS = 256
DECODE_STEPS = 4
CAP = 2
PREFIX_TOKENS = 2048
REQUESTS_PER_DP = 32
REQUEST_TOTAL = 1024
SLOTS = 64
ALL_SLOTS = 2048
N_DP = 32


def draw_prefix_kv(key, part):
    key = jax.random.fold_in(key, 11)
    array_shape = (N_DP * PREFIX_TOKENS, KV_HEAD_COUNT, 2, HEAD_SIZE)
    table_entries = jnp.clip(jax.random.normal(key, array_shape, jnp.float32), -6.0, 6.0)
    return table_entries.reshape(N_DP * PREFIX_TOKENS, KV_HEAD_COUNT * 2 * HEAD_SIZE).astype(jnp.bfloat16)


def draw_decoded_queries(key, part):
    key = jax.random.fold_in(key, 23)
    array_shape = (REQUEST_TOTAL, DECODE_STEPS, QUERY_HEADS, HEAD_SIZE)
    table_entries = jnp.clip(jax.random.normal(key, array_shape, jnp.float32), -6.0, 6.0)
    return table_entries.reshape(REQUEST_TOTAL, DECODE_STEPS, QUERY_HEADS * HEAD_SIZE).astype(jnp.bfloat16)


def draw_assign(key, part):
    key = jax.random.fold_in(key, 37)
    count_of_blocks = REQUEST_TOTAL // REQUESTS_PER_DP
    busiest = jax.random.randint(jax.random.fold_in(key, 1), (), 0, N_DP).astype(jnp.int32)

    def single_block(block_key):
        first_key, second_key = jax.random.split(block_key)
        remaining = jax.random.permutation(first_key, (N_DP - 1) * CAP)[:REQUESTS_PER_DP - CAP] // CAP
        remaining = (remaining + (remaining >= busiest).astype(remaining.dtype)).astype(jnp.int32)
        listing = jnp.concatenate([jnp.zeros((CAP,), jnp.int32) + busiest, remaining])
        return jax.random.permutation(second_key, listing)
    block_keys = jax.random.split(jax.random.fold_in(key, 2), count_of_blocks)
    return jax.vmap(single_block)(block_keys).reshape(REQUEST_TOTAL, 1).astype(jnp.int32)


def place_ends(array, own_key, smallest, largest):
    spot = [jax.random.randint(jax.random.fold_in(own_key, axis), (), 0, length) for axis, length in enumerate(array.shape)]
    main_axis = array.shape.index(max(array.shape))
    next_to = spot[:main_axis] + [(spot[main_axis] + 1) % array.shape[main_axis]] + spot[main_axis + 1:]
    return array.at[tuple(spot)].set(smallest).at[tuple(next_to)].set(largest)


def block_levels(rng, extent, cuts, least, largest):
    def one(dim, shards_of):
        heights = jax.random.uniform(jax.random.fold_in(jax.random.fold_in(rng, 6), dim), (shards_of,), jnp.float32, least / len(cuts), largest / len(cuts))
        return jnp.repeat(jnp.exp(heights), extent[dim] // shards_of).reshape((-1,) + (1,) * (len(extent) - dim - 1))

    loudness = one(*cuts[0])
    for cut in cuts[1:]:
        loudness = loudness * one(*cut)
    return loudness


def scatter_about(key, shape, scale, reach, cuts=(), held_as=jnp.bfloat16):
    drawn = scale * jax.random.normal(key, shape, jnp.float32)
    if cuts:
        drawn = drawn * block_levels(key, shape, cuts, -0.22, 0.18)
    return jnp.clip(drawn, -reach, reach).astype(held_as)


def setup_inputs(seed: int = 0) -> dict:
    key_of = jax.random.split(jax.random.key(seed), 11)
    prefix_kv = draw_prefix_kv(jax.random.fold_in(key_of[10], 71), 0)
    page_key_values = scatter_about(key_of[1], (REQUEST_TOTAL, PAGE_POSITIONS, 2 * KV_HEAD_COUNT * HEAD_SIZE), 1.0, 6.0, ((0, 32), (2, 8)))
    context_len = place_ends(jax.random.randint(key_of[2], (REQUEST_TOTAL,), 1, PAGE_POSITIONS + 1), jax.random.fold_in(key_of[2], 1), 1, PAGE_POSITIONS).astype(jnp.int32)
    prefill_owner = jax.random.randint(key_of[3], (1,), 0, N_DP).astype(jnp.int32)
    assign = draw_assign(jax.random.fold_in(key_of[10], 71), 0)
    x_new = scatter_about(key_of[5], (REQUEST_TOTAL, DECODE_STEPS, MODEL_WIDTH), 1.0, 6.0, ((0, 32), (2, 8)))
    norm_gain = jnp.clip(1.0 + 0.18 * jax.random.normal(key_of[6], (MODEL_WIDTH,), jnp.float32), 0.1, 1.9)
    key_weight = scatter_about(key_of[7], (MODEL_WIDTH, KV_HEAD_COUNT * HEAD_SIZE), (MODEL_WIDTH // 16) ** -0.5, 0.25, ((1, 8),))
    value_weight = scatter_about(key_of[8], (MODEL_WIDTH, KV_HEAD_COUNT * HEAD_SIZE), MODEL_WIDTH ** -0.5, 0.0625, ((1, 8),))
    decoded_queries = draw_decoded_queries(jax.random.fold_in(key_of[10], 71), 0)
    return dict(prefix_kv=prefix_kv, page_key_values=page_key_values, context_len=context_len, prefill_owner=prefill_owner, assign=assign, x_new=x_new, norm_gain=norm_gain, key_weight=key_weight, value_weight=value_weight, decoded_queries=decoded_queries)


epsilon = 1e-05
highest_precision = lax.Precision.HIGHEST

def attend(queries, page_rows, recent_key_values, request_lengths, prefix):
    members = queries.shape[0]
    step_count = queries.shape[1]
    key_heads = prefix.shape[1] // (2 * HEAD_SIZE)
    group_size = queries.shape[2] // (key_heads * HEAD_SIZE)
    page_span = page_rows.shape[1]
    grouped = queries.astype(jnp.float32).reshape(members, step_count, key_heads, group_size, HEAD_SIZE)
    shared = prefix.astype(jnp.float32).reshape(prefix.shape[0], key_heads, 2, HEAD_SIZE)
    paged = page_rows.astype(jnp.float32).reshape(members, page_span, key_heads, 2, HEAD_SIZE)
    recent = recent_key_values.astype(jnp.float32).reshape(members, step_count, key_heads, 2, HEAD_SIZE)
    scaling = 1.0 / math.sqrt(HEAD_SIZE)
    shared_scores = jnp.einsum('ntjgd,ljd->ntjgl', grouped, shared[:, :, 0], precision=highest_precision) * scaling
    paged_scores = jnp.einsum('ntjgd,npjd->ntjgp', grouped, paged[:, :, :, 0], precision=highest_precision) * scaling
    recent_scores = jnp.einsum('ntjgd,nsjd->ntjgs', grouped, recent[:, :, :, 0], precision=highest_precision) * scaling
    position = jnp.arange(page_span).astype(jnp.float32)
    visible = position[None, :] < request_lengths[:, None]
    paged_scores = jnp.where(visible[:, None, None, None, :], paged_scores, -jnp.inf)
    causal = jnp.arange(step_count)[None, :] <= jnp.arange(step_count)[:, None]
    recent_scores = jnp.where(causal[None, :, None, None, :], recent_scores, -jnp.inf)
    highest = jnp.maximum(jnp.maximum(lax.optimization_barrier(jnp.max(shared_scores, axis=-1, keepdims=True)), lax.optimization_barrier(jnp.max(paged_scores, axis=-1, keepdims=True))), lax.optimization_barrier(jnp.max(recent_scores, axis=-1, keepdims=True)))
    shared_exp = jnp.exp(shared_scores - highest)
    paged_exp = jnp.exp(paged_scores - highest)
    recent_exp = jnp.exp(recent_scores - highest)
    denominator = lax.optimization_barrier(jnp.sum(shared_exp, axis=-1, keepdims=True)) + lax.optimization_barrier(jnp.sum(paged_exp, axis=-1, keepdims=True)) + lax.optimization_barrier(jnp.sum(recent_exp, axis=-1, keepdims=True))
    shared_weights = (shared_exp / denominator).astype(jnp.bfloat16).astype(jnp.float32)
    paged_weights = (paged_exp / denominator).astype(jnp.bfloat16).astype(jnp.float32)
    recent_weights = (recent_exp / denominator).astype(jnp.bfloat16).astype(jnp.float32)
    result = jnp.einsum('ntjgl,ljd->ntjgd', shared_weights, shared[:, :, 1], precision=highest_precision)
    result = result + jnp.einsum('ntjgp,npjd->ntjgd', paged_weights, paged[:, :, :, 1], precision=highest_precision)
    result = result + jnp.einsum('ntjgs,nsjd->ntjgd', recent_weights, recent[:, :, :, 1], precision=highest_precision)
    return result.reshape(members, step_count, key_heads * group_size * HEAD_SIZE).astype(jnp.bfloat16)

def reference(prefix_kv, page_key_values, context_len, prefill_owner, assign, x_new, norm_gain, key_weight, value_weight, decoded_queries):
    count_of_blocks = REQUEST_TOTAL // REQUESTS_PER_DP
    features = x_new.astype(jnp.float32)
    normed = (features * lax.rsqrt(lax.optimization_barrier(jnp.mean(features * features, axis=2, keepdims=True)) + epsilon) * norm_gain).astype(jnp.bfloat16)
    flattened = normed.reshape(REQUEST_TOTAL * DECODE_STEPS, MODEL_WIDTH)
    fresh_keys = jnp.dot(flattened, key_weight, preferred_element_type=jnp.float32).astype(jnp.bfloat16)
    fresh_values = jnp.dot(flattened, value_weight, preferred_element_type=jnp.float32).astype(jnp.bfloat16)
    recent_key_values = jnp.stack([fresh_keys.reshape(REQUEST_TOTAL, DECODE_STEPS, KV_HEAD_COUNT, HEAD_SIZE), fresh_values.reshape(REQUEST_TOTAL, DECODE_STEPS, KV_HEAD_COUNT, HEAD_SIZE)], axis=3).reshape(REQUEST_TOTAL, DECODE_STEPS, 2 * KV_HEAD_COUNT * HEAD_SIZE)
    start = (prefill_owner[0] * PREFIX_TOKENS).astype(jnp.int32)
    prefix = lax.dynamic_slice_in_dim(prefix_kv, start, PREFIX_TOKENS, 0)
    request_lengths = context_len.astype(jnp.float32)

    def single_block(pieces):
        return attend(pieces[0], pieces[1], pieces[2], pieces[3], prefix)
    attended_output = lax.map(single_block, (decoded_queries.reshape(count_of_blocks, REQUESTS_PER_DP, DECODE_STEPS, QUERY_HEADS * HEAD_SIZE), page_key_values.reshape(count_of_blocks, REQUESTS_PER_DP, PAGE_POSITIONS, 2 * KV_HEAD_COUNT * HEAD_SIZE), recent_key_values.reshape(count_of_blocks, REQUESTS_PER_DP, DECODE_STEPS, 2 * KV_HEAD_COUNT * HEAD_SIZE), request_lengths.reshape(count_of_blocks, REQUESTS_PER_DP)))
    attended_output = attended_output.reshape(REQUEST_TOTAL, DECODE_STEPS, QUERY_HEADS * HEAD_SIZE)
    assigned = assign[:, 0].reshape(count_of_blocks, REQUESTS_PER_DP)
    indices = jnp.arange(REQUESTS_PER_DP)
    matching = (assigned[:, :, None] == assigned[:, None, :]) & (indices[None, None, :] < indices[None, :, None])
    ranking = lax.optimization_barrier(jnp.sum(matching.astype(jnp.int32), axis=2))
    slot_index = assigned * SLOTS + jnp.arange(count_of_blocks).astype(jnp.int32)[:, None] * CAP + ranking
    decoded = jnp.zeros((ALL_SLOTS, DECODE_STEPS, QUERY_HEADS * HEAD_SIZE), jnp.bfloat16).at[slot_index.reshape(REQUEST_TOTAL).astype(jnp.int32)].set(attended_output)
    return decoded
```

```python
import math

import jax
import jax.numpy as jnp
from jax import lax
from jax.experimental import pallas as pl
from jax.experimental.pallas import tpu as pltpu
from jax.sharding import PartitionSpec as P

HEAD_SIZE = 128
CAP = 2
EPSILON = 1e-05
EXP_SCALE = math.log2(math.e) / math.sqrt(HEAD_SIZE)
VMEM_LIMIT = 40 * 1024 * 1024
Y, Z, CORE, X, PAIR = 4, 4, 2, 4, 2


def y_step(k):
    return [(i, (i + Z * CORE * k) % (Y * Z * CORE)) for i in range(Y * Z * CORE)]


def z_step(k):
    plane = Z * CORE
    return [(i, i // plane * plane + (i % plane + CORE * k) % plane) for i in range(Y * plane)]


def core_swap():
    return [(i, i ^ 1) for i in range(Y * Z * CORE)]


def x_step(k):
    return [(i, (i + PAIR * k) % (X * PAIR)) for i in range(X * PAIR)]


def pair_swap():
    return [(i, i ^ 1) for i in range(X * PAIR)]


def choose(index, options):
    chosen = options[0]
    for i in range(1, len(options)):
        chosen = jnp.where(index == i, options[i], chosen)
    return chosen


def dot_nt(a, b):
    return lax.dot_general(a, b, (((1,), (1,)), ((), ())), preferred_element_type=jnp.float32)


def with_ones(key_values):
    ones = jnp.ones((key_values.shape[0], HEAD_SIZE), key_values.dtype)
    return jnp.concatenate([ones, key_values[:, HEAD_SIZE:]], axis=1)


def weighted(scores, highest, key_values):
    weights = jnp.exp2(scores * EXP_SCALE - highest * EXP_SCALE).astype(jnp.bfloat16)
    return jnp.dot(weights, with_ones(key_values), preferred_element_type=jnp.float32)


def page_kernel(lengths, queries, pages, sums, tops):
    base = pl.program_id(0) * pages.shape[0]
    rows = queries.shape[0] // pages.shape[0]
    span = pages.shape[1]
    for i in range(pages.shape[0]):
        here = slice(i * rows, (i + 1) * rows)
        scores = dot_nt(queries[here, :], pages[i, :, :HEAD_SIZE])
        position = lax.broadcasted_iota(jnp.int32, (rows, span), 1)
        scores = jnp.where(position < lengths[base + i], scores, -jnp.inf)
        highest = jnp.max(scores, axis=1, keepdims=True)
        sums[here, :] = weighted(scores, highest, pages[i])
        tops[here, :] = highest


def page_part(lengths, queries, pages):
    count, span, width = pages.shape
    rows = queries.shape[0]
    batch = 4
    steps = count // batch
    return pl.pallas_call(
        page_kernel,
        grid_spec=pltpu.PrefetchScalarGridSpec(
            num_scalar_prefetch=1,
            grid=(steps,),
            in_specs=[
                pl.BlockSpec((rows // steps, HEAD_SIZE), lambda i, _: (i, 0)),
                pl.BlockSpec((batch, span, width), lambda i, _: (i, 0, 0)),
            ],
            out_specs=[
                pl.BlockSpec((rows // steps, 2 * HEAD_SIZE), lambda i, _: (i, 0)),
                pl.BlockSpec((rows // steps, 1), lambda i, _: (i, 0)),
            ],
        ),
        out_shape=[
            jax.ShapeDtypeStruct((rows, 2 * HEAD_SIZE), jnp.float32),
            jax.ShapeDtypeStruct((rows, 1), jnp.float32),
        ],
        compiler_params=pltpu.CompilerParams(vmem_limit_bytes=VMEM_LIMIT),
        cost_estimate=pl.CostEstimate(
            flops=4 * rows * span * HEAD_SIZE, bytes_accessed=pages.size * 2, transcendentals=rows * span
        ),
    )(lengths, queries, pages)


def prefix_kernel(queries, key_values, sums, tops):
    scores = dot_nt(queries[...], key_values[:, :HEAD_SIZE])
    highest = jnp.max(scores, axis=1, keepdims=True)
    sums[...] = weighted(scores, highest, key_values[...])
    tops[...] = highest


def prefix_part(queries, key_values):
    rows = queries.shape[0]
    span = key_values.shape[0]
    steps = 4
    return pl.pallas_call(
        prefix_kernel,
        grid=(steps,),
        in_specs=[
            pl.BlockSpec((rows // steps, HEAD_SIZE), lambda i: (i, 0)),
            pl.BlockSpec((span, 2 * HEAD_SIZE), lambda i: (0, 0)),
        ],
        out_specs=[
            pl.BlockSpec((rows // steps, 2 * HEAD_SIZE), lambda i: (i, 0)),
            pl.BlockSpec((rows // steps, 1), lambda i: (i, 0)),
        ],
        out_shape=[
            jax.ShapeDtypeStruct((rows, 2 * HEAD_SIZE), jnp.float32),
            jax.ShapeDtypeStruct((rows, 1), jnp.float32),
        ],
        compiler_params=pltpu.CompilerParams(vmem_limit_bytes=VMEM_LIMIT),
        cost_estimate=pl.CostEstimate(
            flops=8 * rows * span * HEAD_SIZE, bytes_accessed=span * 512, transcendentals=rows * span
        ),
    )(queries, key_values)


def projection_kernel(owners, gain, key_weight, value_weight, *refs):
    blocks, out = refs[:-1], refs[-1]
    wide = blocks[0].shape[1]
    tokens = blocks[0].shape[0]
    squares = jnp.zeros((tokens, 1), jnp.float32)
    for block in blocks:
        features = block[...].astype(jnp.float32)
        squares = squares + jnp.sum(features * features, axis=1, keepdims=True)
    scale = lax.rsqrt(squares / (wide * len(blocks)) + EPSILON)
    keys = jnp.zeros((tokens, HEAD_SIZE), jnp.float32)
    values = jnp.zeros((tokens, HEAD_SIZE), jnp.float32)
    for i, block in enumerate(blocks):
        normed = block[...].astype(jnp.float32) * scale * gain[pl.ds(owners[i], 1), :]
        normed = normed.astype(jnp.bfloat16)
        rows = pl.ds(pl.multiple_of(owners[i] * wide, wide), wide)
        keys = keys + jnp.dot(normed, key_weight[rows, :], preferred_element_type=jnp.float32)
        values = values + jnp.dot(normed, value_weight[rows, :], preferred_element_type=jnp.float32)
    out[:, :HEAD_SIZE] = keys.astype(jnp.bfloat16)
    out[:, HEAD_SIZE:] = values.astype(jnp.bfloat16)


def project(owners, gain, key_weight, value_weight, blocks):
    tokens, wide = blocks[0].shape
    vmem = pl.BlockSpec(memory_space=pltpu.VMEM)
    return pl.pallas_call(
        projection_kernel,
        in_specs=[pl.BlockSpec(memory_space=pltpu.SMEM)] + [vmem] * (3 + len(blocks)),
        out_specs=vmem,
        out_shape=jax.ShapeDtypeStruct((tokens, 2 * HEAD_SIZE), jnp.bfloat16),
        compiler_params=pltpu.CompilerParams(vmem_limit_bytes=VMEM_LIMIT),
        cost_estimate=pl.CostEstimate(
            flops=4 * tokens * key_weight.size, bytes_accessed=key_weight.size * 4, transcendentals=0
        ),
    )(owners, gain.reshape(len(blocks), wide), key_weight, value_weight, *blocks)


def merge_kernel(slots, queries, key_values, recent, *refs):
    parts, out = refs[:-1], refs[-1]
    rows = queries.shape[0]
    tokens = recent.shape[0]
    step = pl.program_id(0)
    requests = rows // 32

    @pl.when(step == 0)
    def _():
        out[...] = jnp.zeros_like(out)

    scores = dot_nt(queries[...], key_values[:, :HEAD_SIZE])
    new_scores = dot_nt(queries[...], recent[:, :HEAD_SIZE])
    row = lax.broadcasted_iota(jnp.int32, (rows, tokens), 0)
    token = lax.broadcasted_iota(jnp.int32, (rows, tokens), 1)
    seen = (row // 32 == token // 4) & (token % 4 <= (row % 32) // 8)
    new_scores = jnp.where(seen, new_scores, -jnp.inf)
    highest = jnp.maximum(
        jnp.max(scores, axis=1, keepdims=True), jnp.max(new_scores, axis=1, keepdims=True)
    )
    for top in parts[1::2]:
        highest = jnp.maximum(highest, top[...])
    total = weighted(scores, highest, key_values[...]) + weighted(new_scores, highest, recent[...])
    for sums, top in zip(parts[::2], parts[1::2]):
        total = total + sums[...] * jnp.exp2(top[...] * EXP_SCALE - highest * EXP_SCALE)
    result = (total[:, HEAD_SIZE:] / total[:, :HEAD_SIZE]).astype(jnp.bfloat16)
    for i in range(requests):
        out[slots[step * requests + i]] = result[i * 32 : (i + 1) * 32, :]


def merge(slots, queries, key_values, recent, parts, slot_count):
    rows = queries.shape[0]
    span = key_values.shape[0]
    steps = 4
    part_specs = []
    for part in parts:
        part_specs.append(pl.BlockSpec((rows // steps, part.shape[1]), lambda i, _: (i, 0)))
    return pl.pallas_call(
        merge_kernel,
        grid_spec=pltpu.PrefetchScalarGridSpec(
            num_scalar_prefetch=1,
            grid=(steps,),
            in_specs=[
                pl.BlockSpec((rows // steps, HEAD_SIZE), lambda i, _: (i, 0)),
                pl.BlockSpec((span, 2 * HEAD_SIZE), lambda i, _: (0, 0)),
                pl.BlockSpec((recent.shape[0] // steps, 2 * HEAD_SIZE), lambda i, _: (i, 0)),
            ]
            + part_specs,
            out_specs=pl.BlockSpec((slot_count, 32, HEAD_SIZE), lambda i, _: (0, 0, 0)),
        ),
        out_shape=jax.ShapeDtypeStruct((slot_count, 32, HEAD_SIZE), jnp.bfloat16),
        compiler_params=pltpu.CompilerParams(vmem_limit_bytes=VMEM_LIMIT),
        cost_estimate=pl.CostEstimate(
            flops=8 * rows * span * HEAD_SIZE, bytes_accessed=span * 512, transcendentals=rows * span
        ),
    )(slots, queries, key_values, recent, *parts)


def gather_features(block):
    me = lax.axis_index("tensor")
    x, pair = me // PAIR, me % PAIR
    half = block.shape[0] // 2
    twin = lax.ppermute(block, "tensor", pair_swap())
    left = lax.ppermute(block, "tensor", x_step(1))
    right = lax.ppermute(block, "tensor", x_step(X - 1))
    far_top = lax.ppermute(left[:half], "tensor", x_step(1))
    far_bottom = lax.ppermute(right[half:], "tensor", x_step(X - 1))
    twin_left = lax.ppermute(twin, "tensor", x_step(1))
    twin_right = lax.ppermute(twin, "tensor", x_step(X - 1))
    far = jnp.concatenate([far_top, far_bottom])
    twin_far = lax.ppermute(far, "tensor", pair_swap())
    places = [(0, 0), (0, 1), (X - 1, 0), (1, 0), (X - 1, 1), (1, 1), (2, 0), (2, 1)]
    owners = jnp.stack([(x + dx) % X * PAIR + (pair ^ flip) for dx, flip in places])
    return owners.astype(jnp.int32), [block, twin, left, right, twin_left, twin_right, far, twin_far]


def spread_prefix(block, owner):
    me = lax.axis_index("dp")
    y, z, core = me // (Z * CORE), me // CORE % Z, me % CORE
    own_y, own_z, own_core = owner // (Z * CORE), owner // CORE % Z, owner % CORE
    half = block.shape[0] // 2
    piece = half // Y
    other = lax.ppermute(block[half:], "dp", core_swap())
    mine = jnp.where(core == own_core, block[:half], other)
    arrived = [mine[:piece]]
    for k in range(1, Y):
        arrived.append(lax.ppermute(mine[piece * k : piece * (k + 1)], "dp", y_step(k)))
    part = choose((y - own_y) % Y, arrived)
    part = choose((z - own_z) % Z, [part] + [lax.ppermute(part, "dp", z_step(k)) for k in range(1, Z)])
    near = jnp.concatenate([part] + [lax.ppermute(part, "dp", y_step(k)) for k in range(1, Y)])
    return near, lax.ppermute(near, "dp", core_swap())


def per_device(
    prefix_kv,
    page_key_values,
    context_len,
    prefill_owner,
    assign,
    x_new,
    norm_gain,
    key_weight,
    value_weight,
    decoded_queries,
):
    row_count, step_count, width = decoded_queries.shape
    group_count = lax.axis_size("dp")
    near, far = spread_prefix(prefix_kv, prefill_owner[0])
    owners, blocks = gather_features(x_new.reshape(row_count * step_count, x_new.shape[2]))

    assigned = assign[:, 0]
    indices = jnp.arange(row_count)
    matching = (assigned[:, None] == assigned[None, :]) & (indices[None, :] < indices[:, None])
    slots = assigned * CAP + jnp.sum(matching.astype(jnp.int32), axis=1)

    queries = decoded_queries.reshape(-1, HEAD_SIZE)
    page_sums, page_tops = page_part(context_len, queries, page_key_values)
    recent = project(owners, norm_gain, key_weight, value_weight, blocks)
    near_sums, near_tops = prefix_part(queries, near)
    slot_count = group_count * CAP
    result = merge(
        slots, queries, far, recent, [page_sums, page_tops, near_sums, near_tops], slot_count
    )
    decoded = lax.all_to_all(
        result.reshape(group_count, CAP * 32, HEAD_SIZE), "dp", split_axis=0, concat_axis=0, tiled=True
    )
    return decoded.reshape(slot_count, step_count, width)


def solution(mesh):
    in_specs = (
        P("dp", "tensor"),
        P("dp", None, "tensor"),
        P("dp"),
        P(),
        P("dp", None),
        P("dp", None, "tensor"),
        P(),
        P(None, "tensor"),
        P(None, "tensor"),
        P("dp", None, "tensor"),
    )
    out_specs = P("dp", None, "tensor")
    return jax.shard_map(
        per_device, mesh=mesh, in_specs=in_specs, out_specs=out_specs, check_vma=False
    )
```

```python
import math

import jax
import jax.numpy as jnp
from jax import lax
from jax.experimental import pallas as pl
from jax.experimental.pallas import tpu as pltpu
from jax.sharding import PartitionSpec as P

HEAD_SIZE = 128
CAP = 2
EPSILON = 1e-05
EXP_SCALE = math.log2(math.e) / math.sqrt(HEAD_SIZE)
VMEM_LIMIT = 16 * 1024 * 1024
BLOCK_ROWS = 128
Y, Z, CORE, X, PAIR = 4, 4, 2, 4, 2


def y_step(k):
    return [(i, (i + Z * CORE * k) % (Y * Z * CORE)) for i in range(Y * Z * CORE)]


def z_step(k):
    plane = Z * CORE
    return [(i, i // plane * plane + (i % plane + CORE * k) % plane) for i in range(Y * plane)]


def core_swap():
    return [(i, i ^ 1) for i in range(Y * Z * CORE)]


def x_step(k):
    return [(i, (i + PAIR * k) % (X * PAIR)) for i in range(X * PAIR)]


def pair_swap():
    return [(i, i ^ 1) for i in range(X * PAIR)]


def choose(index, options):
    chosen = options[0]
    for i in range(1, len(options)):
        chosen = jnp.where(index == i, options[i], chosen)
    return chosen


def together(*arrays):
    return lax.optimization_barrier(arrays)


def dot_nt(a, b):
    return lax.dot_general(a, b, (((1,), (1,)), ((), ())), preferred_element_type=jnp.float32)


def with_ones(key_values):
    ones = jnp.ones((key_values.shape[0], HEAD_SIZE), key_values.dtype)
    return jnp.concatenate([ones, key_values[:, HEAD_SIZE:]], axis=1)


def weighted(scores, highest, key_values):
    weights = jnp.exp2(scores * EXP_SCALE - highest * EXP_SCALE).astype(jnp.bfloat16)
    return jnp.dot(weights, with_ones(key_values), preferred_element_type=jnp.float32)


def page_kernel(lengths, queries, pages, sums, tops):
    count, span = pages.shape[:2]
    each = queries.shape[0] // count
    position = lax.broadcasted_iota(jnp.int32, (each, span), 1)
    for request in range(count):
        here = slice(request * each, (request + 1) * each)
        scores = dot_nt(queries[here, :], pages[request, :, :HEAD_SIZE])
        scores = jnp.where(position < lengths[request], scores, -jnp.inf)
        highest = jnp.max(scores, axis=1, keepdims=True)
        sums[here, :] = weighted(scores, highest, pages[request])
        tops[here, :] = highest


def page_part(lengths, queries, pages):
    count, span, width = pages.shape
    rows = queries.shape[0]
    vmem = pl.BlockSpec(memory_space=pltpu.VMEM)
    return pl.pallas_call(
        page_kernel,
        in_specs=[pl.BlockSpec(memory_space=pltpu.SMEM), vmem, vmem],
        out_specs=[vmem] * 2,
        out_shape=[
            jax.ShapeDtypeStruct((rows, 2 * HEAD_SIZE), jnp.float32),
            jax.ShapeDtypeStruct((rows, 1), jnp.float32),
        ],
        compiler_params=pltpu.CompilerParams(vmem_limit_bytes=VMEM_LIMIT),
        cost_estimate=pl.CostEstimate(
            flops=4 * rows * span * HEAD_SIZE, bytes_accessed=pages.size * 2, transcendentals=rows * span
        ),
    )(lengths, queries, pages)


def attend_rows(queries, key_values, sums, tops, here):
    scores = dot_nt(queries[here, :], key_values[:, :HEAD_SIZE])
    before = tops[here, :]
    highest = jnp.maximum(before, jnp.max(scores, axis=1, keepdims=True))
    total = sums[here, :] * jnp.exp2(before * EXP_SCALE - highest * EXP_SCALE)
    return total + weighted(scores, highest, key_values[...]), highest


def prefix_kernel(queries, key_values, sums, tops, new_sums, new_tops):
    for start in range(0, queries.shape[0], BLOCK_ROWS):
        here = slice(start, start + BLOCK_ROWS)
        new_sums[here, :], new_tops[here, :] = attend_rows(queries, key_values, sums, tops, here)


def prefix_part(queries, key_values, sums, tops):
    rows = queries.shape[0]
    span = key_values.shape[0]
    vmem = pl.BlockSpec(memory_space=pltpu.VMEM)
    return pl.pallas_call(
        prefix_kernel,
        in_specs=[vmem] * 4,
        out_specs=[vmem] * 2,
        out_shape=[
            jax.ShapeDtypeStruct(sums.shape, jnp.float32),
            jax.ShapeDtypeStruct(tops.shape, jnp.float32),
        ],
        compiler_params=pltpu.CompilerParams(vmem_limit_bytes=VMEM_LIMIT),
        cost_estimate=pl.CostEstimate(
            flops=8 * rows * span * HEAD_SIZE, bytes_accessed=span * 512, transcendentals=rows * span
        ),
    )(queries, key_values, sums, tops)


def project(owners, gain, key_weight, value_weight, blocks, out):
    tokens, wide = blocks[0].shape
    squares = jnp.zeros((tokens, 1), jnp.float32)
    for block in blocks:
        features = block[...].astype(jnp.float32)
        squares = squares + jnp.sum(features * features, axis=1, keepdims=True)
    scale = lax.rsqrt(squares / (wide * len(blocks)) + EPSILON)
    keys = jnp.zeros((tokens, HEAD_SIZE), jnp.float32)
    values = jnp.zeros((tokens, HEAD_SIZE), jnp.float32)
    for i, block in enumerate(blocks):
        rows = pl.ds(pl.multiple_of(owners[i] * wide, wide), wide)
        normed = block[...].astype(jnp.float32) * scale * gain[:, rows]
        normed = normed.astype(jnp.bfloat16)
        keys = keys + jnp.dot(normed, key_weight[rows, :], preferred_element_type=jnp.float32)
        values = values + jnp.dot(normed, value_weight[rows, :], preferred_element_type=jnp.float32)
    out[:, :HEAD_SIZE] = keys.astype(jnp.bfloat16)
    out[:, HEAD_SIZE:] = values.astype(jnp.bfloat16)


def finish_kernel(slots, owners, gain, key_weight, value_weight, queries, sums, tops, *refs):
    blocks, (out, recent) = refs[:-2], refs[-2:]
    out[...] = jnp.zeros_like(out)
    project(owners, gain, key_weight, value_weight, blocks, recent)
    each = out.shape[1]
    step_tokens = recent.shape[0] * each // queries.shape[0]
    heads = each // step_tokens
    for start in range(0, queries.shape[0], BLOCK_ROWS):
        here = slice(start, start + BLOCK_ROWS)
        scores = dot_nt(queries[here, :], recent[:, :HEAD_SIZE])
        row = lax.broadcasted_iota(jnp.int32, scores.shape, 0) + start
        token = lax.broadcasted_iota(jnp.int32, scores.shape, 1)
        seen = (row // each == token // step_tokens) & (
            token % step_tokens <= row % each // heads
        )
        scores = jnp.where(seen, scores, -jnp.inf)
        before = tops[here, :]
        highest = jnp.maximum(before, jnp.max(scores, axis=1, keepdims=True))
        total = sums[here, :] * jnp.exp2(before * EXP_SCALE - highest * EXP_SCALE)
        total = total + weighted(scores, highest, recent[...])
        result = (total[:, HEAD_SIZE:] / total[:, :HEAD_SIZE]).astype(jnp.bfloat16)
        for i in range(BLOCK_ROWS // each):
            out[slots[start // each + i]] = result[i * each : (i + 1) * each, :]


def finish(slots, owners, gain, key_weight, value_weight, queries, sums, tops, blocks, slot_count):
    rows = queries.shape[0]
    tokens = blocks[0].shape[0]
    vmem = pl.BlockSpec(memory_space=pltpu.VMEM)
    smem = pl.BlockSpec(memory_space=pltpu.SMEM)
    return pl.pallas_call(
        finish_kernel,
        in_specs=[smem, smem] + [vmem] * (6 + len(blocks)),
        out_specs=vmem,
        out_shape=jax.ShapeDtypeStruct((slot_count, rows // slots.shape[0], HEAD_SIZE), jnp.bfloat16),
        scratch_shapes=[pltpu.VMEM((tokens, 2 * HEAD_SIZE), jnp.bfloat16)],
        compiler_params=pltpu.CompilerParams(vmem_limit_bytes=VMEM_LIMIT),
        cost_estimate=pl.CostEstimate(
            flops=4 * tokens * key_weight.size, bytes_accessed=key_weight.size * 4, transcendentals=0
        ),
    )(slots, owners, gain.reshape(1, -1), key_weight, value_weight, queries, sums, tops, *blocks)


def per_device(
    prefix_kv,
    page_key_values,
    context_len,
    prefill_owner,
    assign,
    x_new,
    norm_gain,
    key_weight,
    value_weight,
    decoded_queries,
):
    row_count, step_count, width = decoded_queries.shape
    group_count = lax.axis_size("dp")
    assigned = assign[:, 0]
    indices = jnp.arange(row_count)
    matching = (assigned[:, None] == assigned[None, :]) & (indices[None, :] < indices[:, None])
    slots = assigned * CAP + jnp.sum(matching.astype(jnp.int32), axis=1)

    me, tensor = lax.axis_index("dp"), lax.axis_index("tensor")
    owner = prefill_owner[0]
    y, z, core = me // (Z * CORE), me // CORE % Z, me % CORE
    own_y, own_z, own_core = owner // (Z * CORE), owner // CORE % Z, owner % CORE
    x, pair = tensor // PAIR, tensor % PAIR
    half = prefix_kv.shape[0] // 2
    piece = half // Y
    queries = decoded_queries.reshape(-1, HEAD_SIZE)
    block = x_new.reshape(row_count * step_count, x_new.shape[2])

    other = lax.ppermute(prefix_kv, "dp", core_swap())
    twin = lax.ppermute(block, "tensor", pair_swap())
    left = lax.ppermute(block, "tensor", x_step(1))
    right = lax.ppermute(block, "tensor", x_step(X - 1))
    mine = jnp.where(core == own_core, prefix_kv[:half], other[half:])
    arrived = [mine[:piece]]
    for k in range(1, Y):
        arrived.append(lax.ppermute(mine[piece * k : piece * (k + 1)], "dp", y_step(k)))
    *arrived, twin = together(*arrived, twin)
    part = choose((y - own_y) % Y, arrived)

    page_sums, page_tops = page_part(context_len, queries, page_key_values)
    twin_left = lax.ppermute(twin, "tensor", x_step(1))
    twin_right = lax.ppermute(twin, "tensor", x_step(X - 1))
    far = lax.ppermute(jnp.concatenate([block, twin]), "tensor", x_step(2))
    arrived = [part] + [lax.ppermute(part, "dp", z_step(k)) for k in range(1, Z)]
    *arrived, left, right, twin_left, twin_right, page_sums = together(
        *arrived, left, right, twin_left, twin_right, page_sums
    )
    part = choose((z - own_z) % Z, arrived)

    places = [(0, 0), (0, 1), (X - 1, 0), (1, 0), (X - 1, 1), (1, 1), (2, 0), (2, 1)]
    owners = jnp.stack([(x + dx) % X * PAIR + (pair ^ flip) for dx, flip in places]).astype(jnp.int32)
    tokens = block.shape[0]
    blocks = [block, twin, left, right, twin_left, twin_right, far[:tokens], far[tokens:]]
    arrived = [part] + [lax.ppermute(part, "dp", y_step(k)) for k in range(1, Y)]
    near = jnp.concatenate(arrived)
    far_prefix = lax.ppermute(near, "dp", core_swap())
    sums, tops = prefix_part(queries, near, page_sums, page_tops)
    sums, tops = prefix_part(queries, far_prefix, sums, tops)
    slot_count = group_count * CAP
    result = finish(
        slots, owners, norm_gain, key_weight, value_weight, queries, sums, tops, blocks, slot_count
    )
    decoded = lax.all_to_all(
        result.reshape(group_count, CAP * 32, HEAD_SIZE), "dp", split_axis=0, concat_axis=0, tiled=True
    )
    return decoded.reshape(slot_count, step_count, width)


def solution(mesh):
    in_specs = (
        P("dp", "tensor"),
        P("dp", None, "tensor"),
        P("dp"),
        P(),
        P("dp", None),
        P("dp", None, "tensor"),
        P(),
        P(None, "tensor"),
        P(None, "tensor"),
        P("dp", None, "tensor"),
    )
    out_specs = P("dp", None, "tensor")
    return jax.shard_map(
        per_device, mesh=mesh, in_specs=in_specs, out_specs=out_specs, check_vma=False
    )
```

```python
import math

import jax
import jax.numpy as jnp
from jax import lax
from jax.experimental import pallas as pl
from jax.experimental.pallas import tpu as pltpu
from jax.sharding import PartitionSpec as P

HEAD_SIZE = 128
CAP = 2
EPSILON = 1e-05
EXP_SCALE = math.log2(math.e) / math.sqrt(HEAD_SIZE)
VMEM_LIMIT = 16 * 1024 * 1024
BLOCK_ROWS = 128
Y, Z, CORE, X, PAIR = 4, 4, 2, 4, 2


def y_step(k):
    return [(i, (i + Z * CORE * k) % (Y * Z * CORE)) for i in range(Y * Z * CORE)]


def z_step(k):
    plane = Z * CORE
    return [(i, i // plane * plane + (i % plane + CORE * k) % plane) for i in range(Y * plane)]


def core_swap():
    return [(i, i ^ 1) for i in range(Y * Z * CORE)]


def x_step(k):
    return [(i, (i + PAIR * k) % (X * PAIR)) for i in range(X * PAIR)]


def pair_swap():
    return [(i, i ^ 1) for i in range(X * PAIR)]


def choose(index, options):
    chosen = options[0]
    for i in range(1, len(options)):
        chosen = jnp.where(index == i, options[i], chosen)
    return chosen


def together(*arrays):
    return lax.optimization_barrier(arrays)


def dot_nt(a, b):
    return lax.dot_general(a, b, (((1,), (1,)), ((), ())), preferred_element_type=jnp.float32)


def with_ones(key_values):
    ones = jnp.ones((key_values.shape[0], HEAD_SIZE), key_values.dtype)
    return jnp.concatenate([ones, key_values[:, HEAD_SIZE:]], axis=1)


def weighted(scores, highest, key_values):
    weights = jnp.exp2(scores * EXP_SCALE - highest * EXP_SCALE).astype(jnp.bfloat16)
    return jnp.dot(weights, with_ones(key_values), preferred_element_type=jnp.float32)


def page_kernel(lengths, queries, pages, sums, tops):
    count, span = pages.shape[:2]
    each = queries.shape[0] // count
    position = lax.broadcasted_iota(jnp.int32, (each, span), 1)
    for request in range(count):
        here = slice(request * each, (request + 1) * each)
        scores = dot_nt(queries[here, :], pages[request, :, :HEAD_SIZE])
        scores = jnp.where(position < lengths[request], scores, -jnp.inf)
        highest = jnp.max(scores, axis=1, keepdims=True)
        sums[here, :] = weighted(scores, highest, pages[request])
        tops[here, :] = highest


def page_part(lengths, queries, pages):
    count, span, width = pages.shape
    rows = queries.shape[0]
    vmem = pl.BlockSpec(memory_space=pltpu.VMEM)
    return pl.pallas_call(
        page_kernel,
        in_specs=[pl.BlockSpec(memory_space=pltpu.SMEM), vmem, vmem],
        out_specs=[vmem] * 2,
        out_shape=[
            jax.ShapeDtypeStruct((rows, 2 * HEAD_SIZE), jnp.float32),
            jax.ShapeDtypeStruct((rows, 1), jnp.float32),
        ],
        compiler_params=pltpu.CompilerParams(vmem_limit_bytes=VMEM_LIMIT),
        cost_estimate=pl.CostEstimate(
            flops=4 * rows * span * HEAD_SIZE, bytes_accessed=pages.size * 2, transcendentals=rows * span
        ),
    )(lengths, queries, pages)


def attend_rows(queries, key_values, sums, tops, here):
    scores = dot_nt(queries[here, :], key_values[:, :HEAD_SIZE])
    before = tops[here, :]
    highest = jnp.maximum(before, jnp.max(scores, axis=1, keepdims=True))
    total = sums[here, :] * jnp.exp2(before * EXP_SCALE - highest * EXP_SCALE)
    return total + weighted(scores, highest, key_values[...]), highest


def prefix_kernel(queries, key_values, sums, tops, new_sums, new_tops):
    for start in range(0, queries.shape[0], BLOCK_ROWS):
        here = slice(start, start + BLOCK_ROWS)
        new_sums[here, :], new_tops[here, :] = attend_rows(queries, key_values, sums, tops, here)


def prefix_part(queries, key_values, sums, tops):
    rows = queries.shape[0]
    span = key_values.shape[0]
    vmem = pl.BlockSpec(memory_space=pltpu.VMEM)
    return pl.pallas_call(
        prefix_kernel,
        in_specs=[vmem] * 4,
        out_specs=[vmem] * 2,
        out_shape=[
            jax.ShapeDtypeStruct(sums.shape, jnp.float32),
            jax.ShapeDtypeStruct(tops.shape, jnp.float32),
        ],
        compiler_params=pltpu.CompilerParams(vmem_limit_bytes=VMEM_LIMIT),
        cost_estimate=pl.CostEstimate(
            flops=8 * rows * span * HEAD_SIZE, bytes_accessed=span * 512, transcendentals=rows * span
        ),
    )(queries, key_values, sums, tops)


def project(owners, gain, key_weight, value_weight, blocks, out):
    tokens, wide = blocks[0].shape
    squares = jnp.zeros((tokens, 1), jnp.float32)
    for block in blocks:
        features = block[...].astype(jnp.float32)
        squares = squares + jnp.sum(features * features, axis=1, keepdims=True)
    scale = lax.rsqrt(squares / (wide * len(blocks)) + EPSILON)
    keys = jnp.zeros((tokens, HEAD_SIZE), jnp.float32)
    values = jnp.zeros((tokens, HEAD_SIZE), jnp.float32)
    for i, block in enumerate(blocks):
        rows = pl.ds(pl.multiple_of(owners[i] * wide, wide), wide)
        normed = block[...].astype(jnp.float32) * scale * gain[:, rows]
        normed = normed.astype(jnp.bfloat16)
        keys = keys + jnp.dot(normed, key_weight[rows, :], preferred_element_type=jnp.float32)
        values = values + jnp.dot(normed, value_weight[rows, :], preferred_element_type=jnp.float32)
    out[:, :HEAD_SIZE] = keys.astype(jnp.bfloat16)
    out[:, HEAD_SIZE:] = values.astype(jnp.bfloat16)


def finish_kernel(slots, owners, gain, key_weight, value_weight, queries, sums, tops, *refs):
    (*blocks, far), (out, recent) = refs[:-2], refs[-2:]
    tokens = recent.shape[0]
    blocks = [*blocks, far.at[:tokens], far.at[tokens:]]
    out[...] = jnp.zeros_like(out)
    project(owners, gain, key_weight, value_weight, blocks, recent)
    each = out.shape[1]
    step_tokens = recent.shape[0] * each // queries.shape[0]
    heads = each // step_tokens
    for start in range(0, queries.shape[0], BLOCK_ROWS):
        here = slice(start, start + BLOCK_ROWS)
        scores = dot_nt(queries[here, :], recent[:, :HEAD_SIZE])
        row = lax.broadcasted_iota(jnp.int32, scores.shape, 0) + start
        token = lax.broadcasted_iota(jnp.int32, scores.shape, 1)
        seen = (row // each == token // step_tokens) & (
            token % step_tokens <= row % each // heads
        )
        scores = jnp.where(seen, scores, -jnp.inf)
        before = tops[here, :]
        highest = jnp.maximum(before, jnp.max(scores, axis=1, keepdims=True))
        total = sums[here, :] * jnp.exp2(before * EXP_SCALE - highest * EXP_SCALE)
        total = total + weighted(scores, highest, recent[...])
        result = (total[:, HEAD_SIZE:] / total[:, :HEAD_SIZE]).astype(jnp.bfloat16)
        for i in range(BLOCK_ROWS // each):
            out[slots[start // each + i]] = result[i * each : (i + 1) * each, :]


def finish(slots, owners, gain, key_weight, value_weight, queries, sums, tops, blocks, slot_count):
    rows = queries.shape[0]
    tokens = blocks[0].shape[0]
    vmem = pl.BlockSpec(memory_space=pltpu.VMEM)
    smem = pl.BlockSpec(memory_space=pltpu.SMEM)
    return pl.pallas_call(
        finish_kernel,
        in_specs=[smem, smem] + [vmem] * (6 + len(blocks)),
        out_specs=vmem,
        out_shape=jax.ShapeDtypeStruct((slot_count, rows // slots.shape[0], HEAD_SIZE), jnp.bfloat16),
        scratch_shapes=[pltpu.VMEM((tokens, 2 * HEAD_SIZE), jnp.bfloat16)],
        compiler_params=pltpu.CompilerParams(vmem_limit_bytes=VMEM_LIMIT),
        cost_estimate=pl.CostEstimate(
            flops=4 * tokens * key_weight.size, bytes_accessed=key_weight.size * 4, transcendentals=0
        ),
    )(slots, owners, gain.reshape(1, -1), key_weight, value_weight, queries, sums, tops, *blocks)


def per_device(
    prefix_kv,
    page_key_values,
    context_len,
    prefill_owner,
    assign,
    x_new,
    norm_gain,
    key_weight,
    value_weight,
    decoded_queries,
):
    row_count, step_count, width = decoded_queries.shape
    group_count = lax.axis_size("dp")
    assigned = assign[:, 0]
    indices = jnp.arange(row_count)
    matching = (assigned[:, None] == assigned[None, :]) & (indices[None, :] < indices[:, None])
    slots = assigned * CAP + jnp.sum(matching.astype(jnp.int32), axis=1)

    me, tensor = lax.axis_index("dp"), lax.axis_index("tensor")
    owner = prefill_owner[0]
    y, z, core = me // (Z * CORE), me // CORE % Z, me % CORE
    own_y, own_z, own_core = owner // (Z * CORE), owner // CORE % Z, owner % CORE
    x, pair = tensor // PAIR, tensor % PAIR
    half = prefix_kv.shape[0] // 2
    piece = half // Y
    queries = decoded_queries.reshape(-1, HEAD_SIZE)
    block = x_new.reshape(row_count * step_count, x_new.shape[2])

    other = lax.ppermute(prefix_kv, "dp", core_swap())
    twin = lax.ppermute(block, "tensor", pair_swap())
    left = lax.ppermute(block, "tensor", x_step(1))
    right = lax.ppermute(block, "tensor", x_step(X - 1))
    mine = jnp.where(core == own_core, prefix_kv[:half], other[half:])
    arrived = [mine[:piece]]
    for k in range(1, Y):
        arrived.append(lax.ppermute(mine[piece * k : piece * (k + 1)], "dp", y_step(k)))
    *arrived, twin = together(*arrived, twin)
    part = choose((y - own_y) % Y, arrived)

    page_sums, page_tops = page_part(context_len, queries, page_key_values)
    twin_left = lax.ppermute(twin, "tensor", x_step(1))
    twin_right = lax.ppermute(twin, "tensor", x_step(X - 1))
    far = lax.ppermute(jnp.concatenate([block, twin]), "tensor", x_step(2))
    arrived = [part] + [lax.ppermute(part, "dp", z_step(k)) for k in range(1, Z)]
    *arrived, left, right, page_sums = together(*arrived, left, right, page_sums)
    part = choose((z - own_z) % Z, arrived)

    places = [(0, 0), (0, 1), (X - 1, 0), (1, 0), (X - 1, 1), (1, 1), (2, 0), (2, 1)]
    owners = jnp.stack([(x + dx) % X * PAIR + (pair ^ flip) for dx, flip in places]).astype(jnp.int32)
    arrived = [part] + [lax.ppermute(part, "dp", y_step(k)) for k in range(1, Y)]
    arrived[1], twin_left, twin_right, far = together(arrived[1], twin_left, twin_right, far)
    blocks = [block, twin, left, right, twin_left, twin_right, far]
    near = jnp.concatenate(arrived)
    far_prefix = lax.ppermute(near, "dp", core_swap())
    sums, tops = prefix_part(queries, near, page_sums, page_tops)
    sums, tops = prefix_part(queries, far_prefix, sums, tops)
    slot_count = group_count * CAP
    result = finish(
        slots, owners, norm_gain, key_weight, value_weight, queries, sums, tops, blocks, slot_count
    )
    decoded = lax.all_to_all(
        result.reshape(group_count, CAP * 32, HEAD_SIZE), "dp", split_axis=0, concat_axis=0, tiled=True
    )
    return decoded.reshape(slot_count, step_count, width)


def solution(mesh):
    in_specs = (
        P("dp", "tensor"),
        P("dp", None, "tensor"),
        P("dp"),
        P(),
        P("dp", None),
        P("dp", None, "tensor"),
        P(),
        P(None, "tensor"),
        P(None, "tensor"),
        P("dp", None, "tensor"),
    )
    out_specs = P("dp", None, "tensor")
    return jax.shard_map(
        per_device, mesh=mesh, in_specs=in_specs, out_specs=out_specs, check_vma=False
    )
```

```python
import math

import jax
import jax.numpy as jnp
from jax import lax
from jax.experimental import pallas as pl
from jax.experimental.pallas import tpu as pltpu
from jax.sharding import PartitionSpec as P

HEAD_SIZE = 128
CAP = 2
EPSILON = 1e-05
EXP_SCALE = math.log2(math.e) / math.sqrt(HEAD_SIZE)
VMEM_LIMIT = 16 * 1024 * 1024
BLOCK_ROWS = 128
Y, Z, CORE, X, PAIR = 4, 4, 2, 4, 2


def y_step(k):
    return [(i, (i + Z * CORE * k) % (Y * Z * CORE)) for i in range(Y * Z * CORE)]


def z_step(k):
    plane = Z * CORE
    return [(i, i // plane * plane + (i % plane + CORE * k) % plane) for i in range(Y * plane)]


def core_swap():
    return [(i, i ^ 1) for i in range(Y * Z * CORE)]


def x_step(k):
    return [(i, (i + PAIR * k) % (X * PAIR)) for i in range(X * PAIR)]


def pair_swap():
    return [(i, i ^ 1) for i in range(X * PAIR)]


def choose(index, options):
    chosen = options[0]
    for i in range(1, len(options)):
        chosen = jnp.where(index == i, options[i], chosen)
    return chosen


def together(*arrays):
    return lax.optimization_barrier(arrays)


def dot_nt(a, b):
    return lax.dot_general(a, b, (((1,), (1,)), ((), ())), preferred_element_type=jnp.float32)


def with_ones(key_values):
    ones = jnp.ones((key_values.shape[0], HEAD_SIZE), key_values.dtype)
    return jnp.concatenate([ones, key_values[:, HEAD_SIZE:]], axis=1)


def weighted(scores, highest, key_values):
    weights = jnp.exp2(scores * EXP_SCALE - highest * EXP_SCALE).astype(jnp.bfloat16)
    return jnp.dot(weights, with_ones(key_values), preferred_element_type=jnp.float32)


def page_kernel(lengths, queries, pages, sums, tops):
    count, span = pages.shape[:2]
    each = queries.shape[0] // count
    position = lax.broadcasted_iota(jnp.int32, (each, span), 1)
    for request in range(count):
        here = slice(request * each, (request + 1) * each)
        scores = dot_nt(queries[here, :], pages[request, :, :HEAD_SIZE])
        scores = jnp.where(position < lengths[request], scores, -jnp.inf)
        highest = jnp.max(scores, axis=1, keepdims=True)
        sums[here, :] = weighted(scores, highest, pages[request])
        tops[here, :] = highest


def page_part(lengths, queries, pages):
    count, span, width = pages.shape
    rows = queries.shape[0]
    vmem = pl.BlockSpec(memory_space=pltpu.VMEM)
    return pl.pallas_call(
        page_kernel,
        in_specs=[pl.BlockSpec(memory_space=pltpu.SMEM), vmem, vmem],
        out_specs=[vmem] * 2,
        out_shape=[
            jax.ShapeDtypeStruct((rows, 2 * HEAD_SIZE), jnp.float32),
            jax.ShapeDtypeStruct((rows, 1), jnp.float32),
        ],
        compiler_params=pltpu.CompilerParams(vmem_limit_bytes=VMEM_LIMIT),
        cost_estimate=pl.CostEstimate(
            flops=4 * rows * span * HEAD_SIZE, bytes_accessed=pages.size * 2, transcendentals=rows * span
        ),
    )(lengths, queries, pages)


def attend_rows(queries, key_values, sums, tops, here):
    scores = dot_nt(queries[here, :], key_values[:, :HEAD_SIZE])
    before = tops[here, :]
    highest = jnp.maximum(before, jnp.max(scores, axis=1, keepdims=True))
    total = sums[here, :] * jnp.exp2(before * EXP_SCALE - highest * EXP_SCALE)
    return total + weighted(scores, highest, key_values[...]), highest


def prefix_kernel(queries, key_values, sums, tops, new_sums, new_tops):
    for start in range(0, queries.shape[0], BLOCK_ROWS):
        here = slice(start, start + BLOCK_ROWS)
        new_sums[here, :], new_tops[here, :] = attend_rows(queries, key_values, sums, tops, here)


def prefix_part(queries, key_values, sums, tops):
    rows = queries.shape[0]
    span = key_values.shape[0]
    vmem = pl.BlockSpec(memory_space=pltpu.VMEM)
    return pl.pallas_call(
        prefix_kernel,
        in_specs=[vmem] * 4,
        out_specs=[vmem] * 2,
        out_shape=[
            jax.ShapeDtypeStruct(sums.shape, jnp.float32),
            jax.ShapeDtypeStruct(tops.shape, jnp.float32),
        ],
        compiler_params=pltpu.CompilerParams(vmem_limit_bytes=VMEM_LIMIT),
        cost_estimate=pl.CostEstimate(
            flops=8 * rows * span * HEAD_SIZE, bytes_accessed=span * 512, transcendentals=rows * span
        ),
    )(queries, key_values, sums, tops)


def project(owners, gain, key_weight, value_weight, blocks, out):
    tokens, wide = blocks[0].shape
    squares = jnp.zeros((tokens, 1), jnp.float32)
    for block in blocks:
        features = block[...].astype(jnp.float32)
        squares = squares + jnp.sum(features * features, axis=1, keepdims=True)
    scale = lax.rsqrt(squares / (wide * len(blocks)) + EPSILON)
    keys = jnp.zeros((tokens, HEAD_SIZE), jnp.float32)
    values = jnp.zeros((tokens, HEAD_SIZE), jnp.float32)
    for i, block in enumerate(blocks):
        rows = pl.ds(pl.multiple_of(owners[i] * wide, wide), wide)
        normed = block[...].astype(jnp.float32) * scale * gain[:, rows]
        normed = normed.astype(jnp.bfloat16)
        keys = keys + jnp.dot(normed, key_weight[rows, :], preferred_element_type=jnp.float32)
        values = values + jnp.dot(normed, value_weight[rows, :], preferred_element_type=jnp.float32)
    out[:, :HEAD_SIZE] = keys.astype(jnp.bfloat16)
    out[:, HEAD_SIZE:] = values.astype(jnp.bfloat16)


def finish_kernel(slots, owners, gain, key_weight, value_weight, queries, sums, tops, *refs):
    (*blocks, far), (out, recent) = refs[:-2], refs[-2:]
    tokens = recent.shape[0]
    blocks = [*blocks, far.at[:tokens], far.at[tokens:]]
    out[...] = jnp.zeros_like(out)
    project(owners, gain, key_weight, value_weight, blocks, recent)
    each = out.shape[1]
    step_tokens = recent.shape[0] * each // queries.shape[0]
    heads = each // step_tokens
    for start in range(0, queries.shape[0], BLOCK_ROWS):
        here = slice(start, start + BLOCK_ROWS)
        scores = dot_nt(queries[here, :], recent[:, :HEAD_SIZE])
        row = lax.broadcasted_iota(jnp.int32, scores.shape, 0) + start
        token = lax.broadcasted_iota(jnp.int32, scores.shape, 1)
        seen = (row // each == token // step_tokens) & (
            token % step_tokens <= row % each // heads
        )
        scores = jnp.where(seen, scores, -jnp.inf)
        before = tops[here, :]
        highest = jnp.maximum(before, jnp.max(scores, axis=1, keepdims=True))
        total = sums[here, :] * jnp.exp2(before * EXP_SCALE - highest * EXP_SCALE)
        total = total + weighted(scores, highest, recent[...])
        result = (total[:, HEAD_SIZE:] / total[:, :HEAD_SIZE]).astype(jnp.bfloat16)
        for i in range(BLOCK_ROWS // each):
            out[slots[start // each + i]] = result[i * each : (i + 1) * each, :]


def finish(slots, owners, gain, key_weight, value_weight, queries, sums, tops, blocks, slot_count):
    rows = queries.shape[0]
    tokens = blocks[0].shape[0]
    vmem = pl.BlockSpec(memory_space=pltpu.VMEM)
    smem = pl.BlockSpec(memory_space=pltpu.SMEM)
    return pl.pallas_call(
        finish_kernel,
        in_specs=[smem, smem] + [vmem] * (6 + len(blocks)),
        out_specs=vmem,
        out_shape=jax.ShapeDtypeStruct((slot_count, rows // slots.shape[0], HEAD_SIZE), jnp.bfloat16),
        scratch_shapes=[pltpu.VMEM((tokens, 2 * HEAD_SIZE), jnp.bfloat16)],
        compiler_params=pltpu.CompilerParams(vmem_limit_bytes=VMEM_LIMIT),
        cost_estimate=pl.CostEstimate(
            flops=4 * tokens * key_weight.size, bytes_accessed=key_weight.size * 4, transcendentals=0
        ),
    )(slots, owners, gain.reshape(1, -1), key_weight, value_weight, queries, sums, tops, *blocks)


def per_device(
    prefix_kv,
    page_key_values,
    context_len,
    prefill_owner,
    assign,
    x_new,
    norm_gain,
    key_weight,
    value_weight,
    decoded_queries,
):
    row_count, step_count, width = decoded_queries.shape
    group_count = lax.axis_size("dp")
    assigned = assign[:, 0]
    indices = jnp.arange(row_count)
    matching = (assigned[:, None] == assigned[None, :]) & (indices[None, :] < indices[:, None])
    slots = assigned * CAP + jnp.sum(matching.astype(jnp.int32), axis=1)

    me, tensor = lax.axis_index("dp"), lax.axis_index("tensor")
    owner = prefill_owner[0]
    y, z, core = me // (Z * CORE), me // CORE % Z, me % CORE
    own_y, own_z, own_core = owner // (Z * CORE), owner // CORE % Z, owner % CORE
    x, pair = tensor // PAIR, tensor % PAIR
    half = prefix_kv.shape[0] // 2
    piece = half // Y
    queries = decoded_queries.reshape(-1, HEAD_SIZE)
    block = x_new.reshape(row_count * step_count, x_new.shape[2])

    other = lax.ppermute(prefix_kv, "dp", core_swap())
    twin = lax.ppermute(block, "tensor", pair_swap())
    left = lax.ppermute(block, "tensor", x_step(1))
    right = lax.ppermute(block, "tensor", x_step(X - 1))
    mine = jnp.where(core == own_core, prefix_kv[:half], other[half:])
    arrived = [mine[:piece]]
    for k in range(1, Y):
        arrived.append(lax.ppermute(mine[piece * k : piece * (k + 1)], "dp", y_step(k)))
    *arrived, twin = together(*arrived, twin)
    part = choose((y - own_y) % Y, arrived)

    page_sums, page_tops = page_part(context_len, queries, page_key_values)
    twin_left = lax.ppermute(twin, "tensor", x_step(1))
    twin_right = lax.ppermute(twin, "tensor", x_step(X - 1))
    far = lax.ppermute(jnp.concatenate([block, twin]), "tensor", x_step(2))
    arrived = [part] + [lax.ppermute(part, "dp", z_step(k)) for k in range(1, Z)]
    *arrived, left, right, page_sums = together(*arrived, left, right, page_sums)
    part = choose((z - own_z) % Z, arrived)

    places = [(0, 0), (0, 1), (X - 1, 0), (1, 0), (X - 1, 1), (1, 1), (2, 0), (2, 1)]
    owners = jnp.stack([(x + dx) % X * PAIR + (pair ^ flip) for dx, flip in places]).astype(jnp.int32)
    arrived = [part] + [lax.ppermute(part, "dp", y_step(k)) for k in range(1, Y)]
    arrived[3], twin_left, twin_right, far = together(arrived[3], twin_left, twin_right, far)
    blocks = [block, twin, left, right, twin_left, twin_right, far]
    near = jnp.concatenate(arrived)
    far_prefix = lax.ppermute(near, "dp", core_swap())
    sums, tops = prefix_part(queries, near, page_sums, page_tops)
    sums, tops = prefix_part(queries, far_prefix, sums, tops)
    slot_count = group_count * CAP
    result = finish(
        slots, owners, norm_gain, key_weight, value_weight, queries, sums, tops, blocks, slot_count
    )
    decoded = lax.all_to_all(
        result.reshape(group_count, CAP * 32, HEAD_SIZE), "dp", split_axis=0, concat_axis=0, tiled=True
    )
    return decoded.reshape(slot_count, step_count, width)


def solution(mesh):
    in_specs = (
        P("dp", "tensor"),
        P("dp", None, "tensor"),
        P("dp"),
        P(),
        P("dp", None),
        P("dp", None, "tensor"),
        P(),
        P(None, "tensor"),
        P(None, "tensor"),
        P("dp", None, "tensor"),
    )
    out_specs = P("dp", None, "tensor")
    return jax.shard_map(
        per_device, mesh=mesh, in_specs=in_specs, out_specs=out_specs, check_vma=False
    )
```
